32 devices in a mesh: groups: 2 (over x), shard: 8 (over z, y), replica: 2 (over core).
Axes of the slice: x: 2, y: 2, z: 4, core: 2. Of those that a mesh axis runs over, the one named last changes fastest.
Arguments:
- features: bfloat16 [16384, 5120], P(('groups', 'shard', 'replica')), parts along dimension 0, may hold values from -6 to 6
- cotangents: bfloat16 [16384, 2048], P(('groups', 'shard', 'replica')), parts along dimension 0, may hold values from -6 to 6
- feedback: float32 [2, 10240, 2048], P('replica', ('groups', 'shard')), parts along dimension 1, may hold values from -2 to 2
- factors: float32 [16, 2, 32, 1024], P(('groups', 'shard')), parts along dimension 0, may hold values from -0.1875 to 0.1875
Outputs:
- update: float32 [10240, 2048], P(('groups', 'shard')), parts along dimension 0
- new_feedback: float32 [2, 10240, 2048], P('replica', ('groups', 'shard')), parts along dimension 1
- next_factors: float32 [16, 2, 32, 1024], P(('groups', 'shard')), parts along dimension 0
The draws below stay inside these ranges and needn't reach their ends.
There are 2 independent parts, one for each index of `groups`. The reference program is written for one: setup_inputs(seed, part) draws one part's arguments, and reference() takes and returns one part's arrays. A program takes and returns all parts, laid end to end along the dimension named above; each array names one. Nothing has to cross between parts.
All inputs are finite; a program needn't handle non-finite values.
Results may differ from the reference program's by a relative error of at most 0.012.
Values may be sent and summed in bfloat16 or wider, within the bound.
A program may use at most 128 MiB of HBM per device.

```python
import math
import jax
import jax.numpy as jnp
from jax import lax

D = 5120
KV = 1024
RANK = 32
TOK_DEV = 512
TOKENS = 8192
N_SHARD = 8
N_REPLICA = 2


def with_spikes(array, key, source, target, parts, factor):
    owner, partner = [(jnp.arange(array.shape[axis_at]) // (array.shape[axis_at] // parts)).reshape([-1 if axis == axis_at else 1 for axis in range(array.ndim)]) for axis_at in (source, target)]
    chosen = jax.random.permutation(key, parts)[partner]
    strong = (owner == chosen) | (owner == (partner + parts // 2) % parts)
    return jnp.where(strong, factor * array, array)


def steps_of(stream_key, shape, cuts, low, largest):
    level = 1.0
    for dim, parts in cuts:
        heights = jax.random.uniform(jax.random.fold_in(jax.random.fold_in(stream_key, 6), dim), (parts,), jnp.float32, low / len(cuts), largest / len(cuts))
        level = level * jnp.repeat(jnp.exp(heights), shape[dim] // parts).reshape((-1,) + (1,) * (len(shape) - 1 - dim))
    return level


def bell_draw(rng, extent, width, bound, cuts=(), held_as=jnp.bfloat16):
    gain = steps_of(rng, extent, cuts, -0.22, 0.18) if cuts else 1.0
    drawn = jax.random.normal(rng, extent, jnp.float32) * width * gain
    return jnp.minimum(jnp.maximum(drawn, -bound), bound).astype(held_as)


def heavy_noise(key, dims, spread, bound, cuts, heavy, kind=jnp.bfloat16):
    entries = spread * jax.random.normal(key, dims, jnp.float32)
    if cuts:
        entries = entries * steps_of(key, dims, cuts, -0.22, 0.18)
    return jnp.clip(with_spikes(entries, jax.random.fold_in(key, 3), *heavy), -bound, bound).astype(kind)


def setup_inputs(seed: int = 0, part: int = 0) -> dict:
    key_list = jax.random.split(jax.random.key(seed), 5)
    part_splits = jax.random.split(jax.random.fold_in(key_list[4], part), 5)
    return {
        "features": heavy_noise(part_splits[0], (TOKENS, D), 1.0, 6.0, ((0, 16),), (0, 1, 16, 2.0)),
        "cotangents": bell_draw(part_splits[1], (TOKENS, 2 * KV), 1.0, 6.0, ((0, 16),)),
        "feedback": bell_draw(part_splits[2], (N_REPLICA, D, 2 * KV), 0.25, 2.0, ((0, 2), (1, 8)), jnp.float32),
        "factors": bell_draw(part_splits[3], (N_SHARD, 2, RANK, KV), KV ** -0.5, 0.1875, ((0, 8),), jnp.float32),
    }


def orthonormal(left):
    gram = jnp.einsum('...dq,...dp->...qp', left, left, precision=lax.Precision.HIGHEST)
    lower_part = jnp.linalg.cholesky(gram)
    return lax.linalg.triangular_solve(lower_part, left, left_side=False, lower=True, transpose_a=True)

def reference(features, cotangents, feedback, factors):
    grad_scale = 0.25 / math.sqrt(TOK_DEV * N_SHARD)
    feature_blocks = features.reshape(N_SHARD, N_REPLICA, TOK_DEV, D)
    cotangent_blocks = cotangents.reshape(N_SHARD, N_REPLICA, TOK_DEV, 2 * KV)
    gradient = jnp.zeros((N_REPLICA, D, 2 * KV), jnp.float32)
    for position in range(N_SHARD):
        term = jnp.einsum('rtd,rtc->rdc', feature_blocks[position].astype(jnp.float32), cotangent_blocks[position].astype(jnp.float32))
        rounded = lax.optimization_barrier((term * grad_scale).astype(jnp.bfloat16))
        gradient = gradient + rounded.astype(jnp.float32)
    merged = feedback + gradient
    blocks = merged.reshape(N_REPLICA, N_SHARD, D // N_SHARD, 2, KV)
    left = jnp.einsum('rsdmk,smqk->smdq', blocks, factors, precision=lax.Precision.HIGHEST)
    basis = orthonormal(left)
    next_factors = jnp.einsum('smdq,rsdmk->smqk', basis, blocks, precision=lax.Precision.HIGHEST)
    update = jnp.einsum('smdq,smqk->sdmk', basis, next_factors, precision=lax.Precision.HIGHEST) / N_REPLICA
    update = update.reshape(D, 2 * KV)
    new_feedback = merged - update[None]
    return (update, new_feedback, next_factors)
```

```python
import functools
import math

import jax
import jax.numpy as jnp
from jax import lax
from jax.experimental import pallas as pl
from jax.experimental.pallas import tpu as pltpu
from jax.sharding import PartitionSpec as P

COLS = 256
MESH = pl.DeviceIdType.MESH


def orthonormal(left):
    gram = jnp.einsum("...dq,...dp->...qp", left, left, precision=lax.Precision.HIGHEST)
    lower_part = jnp.linalg.cholesky(gram)
    return lax.linalg.triangular_solve(
        lower_part, left, left_side=False, lower=True, transpose_a=True
    )


def merge_kernel(
    lines, scale, by_slice, x_ref, g_ref, fb_ref, out_ref, xb, gb, up, down, acc,
    sx_loc, sg_loc, sf_loc, sx_send, sx_recv, sg_send, sg_recv,
    up_send, up_recv, down_send, down_recv, out_sem,
):
    tok = g_ref.shape[0]
    rows = xb.shape[2]
    chunks = gb.shape[0]
    last = lines - 1
    me = lax.axis_index("shard")
    z = me // 2
    y = me % 2
    mate = {"shard": me + 1 - 2 * y}
    above = {"shard": jnp.minimum(me + 2, 2 * lines - 2 + y)}
    below = {"shard": jnp.maximum(me - 2, y)}
    lower = z <= last - z
    edge = jnp.minimum(z, last - z)

    def x_part(block):
        if by_slice:
            return x_ref.at[:, pl.ds(pl.multiple_of(block * rows, rows), rows)]
        return x_ref.at[block]

    def g_part(c):
        return g_ref.at[:, pl.ds(pl.multiple_of(c * COLS, COLS), COLS)]

    def x_local(d):
        return pltpu.make_async_copy(
            x_part(2 * d + y), xb.at[d, pl.ds(0, tok)], sx_loc.at[d])

    def x_remote(d):
        return pltpu.make_async_remote_copy(
            src_ref=x_part(2 * d + 1 - y), dst_ref=xb.at[d, pl.ds(tok, tok)],
            send_sem=sx_send.at[d], recv_sem=sx_recv.at[d],
            device_id=mate, device_id_type=MESH)

    def g_local(c):
        return pltpu.make_async_copy(g_part(c), gb.at[c, pl.ds(0, tok)], sg_loc.at[c])

    def g_remote(c):
        return pltpu.make_async_remote_copy(
            src_ref=g_part(c), dst_ref=gb.at[c, pl.ds(tok, tok)],
            send_sem=sg_send.at[c], recv_sem=sg_recv.at[c],
            device_id=mate, device_id_type=MESH)

    def hop(slots, send, recv, d, c, i, target):
        return pltpu.make_async_remote_copy(
            src_ref=slots.at[d, c], dst_ref=slots.at[d, c],
            send_sem=send.at[i % 2], recv_sem=recv.at[d, c],
            device_id=target, device_id_type=MESH)

    def up_hop(i):
        return hop(up, up_send, up_recv, last - i // chunks, i % chunks, i, above)

    def down_hop(i):
        return hop(down, down_send, down_recv, i // chunks, i % chunks, i, below)

    fb_copy = pltpu.make_async_copy(fb_ref.at[0], acc, sf_loc)

    barrier = pltpu.get_barrier_semaphore()
    pl.semaphore_signal(barrier, inc=1, device_id=mate, device_id_type=MESH)

    @pl.when(z < last)
    def _():
        pl.semaphore_signal(barrier, inc=1, device_id=above, device_id_type=MESH)

    @pl.when(z > 0)
    def _():
        pl.semaphore_signal(barrier, inc=1, device_id=below, device_id_type=MESH)

    pl.semaphore_wait(
        barrier, 1 + jnp.where(z < last, 1, 0) + jnp.where(z > 0, 1, 0))

    def start_x(d):
        x_remote(d).start()
        x_local(d).start()

    def start_g(c):
        g_remote(c).start()
        g_local(c).start()

    first = jnp.where(lower, last, 0)
    second = jnp.where(lower, 0, last)
    start_x(first)
    start_g(0)

    @pl.when(edge > 0)
    def _():
        start_x(second)

    @pl.loop(1, chunks)
    def _(c):
        start_g(c)

    @pl.loop(1, last)
    def _(k):
        @pl.when(last - k > z)
        def _():
            start_x(last - k)

        @pl.when(k < z)
        def _():
            start_x(k)

    start_x(z)
    fb_copy.start()

    def wait_x(d):
        x_local(d).wait()
        x_remote(d).wait()

    def term(d, c):
        return lax.dot_general(
            xb[d], gb[c], (((0,), (0,)), ((), ())),
            preferred_element_type=jnp.float32) * scale

    def relay(slots, make, sends, i, d, c, inner):
        @pl.when(c == 0)
        def _():
            wait_x(d)

        value = term(d, c)

        @pl.when(i >= 2)
        def _():
            make(i - 2).wait_send()

        @pl.when(inner)
        def _():
            make(i).wait_recv()
            slots[d, c] = (value + slots[d, c].astype(jnp.float32)).astype(slots.dtype)

        @pl.when(jnp.logical_not(inner))
        def _():
            slots[d, c] = value.astype(slots.dtype)

        make(i).start()

    @pl.loop(edge, last * chunks + last)
    def _(t):
        @pl.when(t - edge < chunks)
        def _():
            g_local(t - edge).wait()
            g_remote(t - edge).wait()

        i = t - z

        @pl.when(jnp.logical_and(i >= 0, i < (last - z) * chunks))
        def _():
            relay(up, up_hop, up_send, i, last - i // chunks, i % chunks, z > 0)

        j = t - (last - z)

        @pl.when(jnp.logical_and(j >= 0, j < z * chunks))
        def _():
            relay(down, down_hop, down_send, j, j // chunks, j % chunks, z < last)

    wait_x(z)
    fb_copy.wait()

    def out_copy(c):
        view = pl.ds(pl.multiple_of(c * COLS, COLS), COLS)
        return pltpu.make_async_copy(
            acc.at[:, view], out_ref.at[:, view], out_sem.at[c])

    @pl.loop(0, chunks)
    def _(c):
        view = pl.ds(pl.multiple_of(c * COLS, COLS), COLS)
        acc[:, view] += term(z, c)

        @pl.when(z > 0)
        def _():
            up_hop((last - z) * chunks + c).wait_recv()
            acc[:, view] += up[z, c].astype(jnp.float32)

        @pl.when(z < last)
        def _():
            down_hop(z * chunks + c).wait_recv()
            acc[:, view] += down[z, c].astype(jnp.float32)

        out_copy(c).start()

    @pl.loop(0, 2)
    def _(k):
        @pl.when(z < last)
        def _():
            up_hop((last - z) * chunks - 2 + k).wait_send()

        @pl.when(z > 0)
        def _():
            down_hop(z * chunks - 2 + k).wait_send()

    @pl.loop(0, chunks)
    def _(c):
        out_copy(c).wait()


def merged_gradient(features, cotangents, feedback, scale):
    shard_count = lax.axis_size("shard")
    lines = shard_count // 2
    tok, width = cotangents.shape
    rows = features.shape[1] // shard_count
    chunks = width // COLS
    by_slice = rows % 128 == 0
    if not by_slice:
        features = features.reshape(tok, shard_count, rows).transpose(1, 0, 2)
    dma = pltpu.SemaphoreType.DMA
    bf16 = jnp.bfloat16
    flops = 2 * tok * rows * shard_count * width
    return pl.pallas_call(
        functools.partial(merge_kernel, lines, scale, by_slice),
        out_shape=jax.ShapeDtypeStruct((rows, width), jnp.float32),
        in_specs=[pl.BlockSpec(memory_space=pl.ANY)] * 3,
        out_specs=pl.BlockSpec(memory_space=pl.ANY),
        scratch_shapes=[
            pltpu.VMEM((lines, 2 * tok, rows), bf16),
            pltpu.VMEM((chunks, 2 * tok, COLS), bf16),
            pltpu.VMEM((lines, chunks, rows, COLS), bf16),
            pltpu.VMEM((lines, chunks, rows, COLS), bf16),
            pltpu.VMEM((rows, width), jnp.float32),
            dma((lines,)), dma((chunks,)), dma,
            dma((lines,)), dma((lines,)), dma((chunks,)), dma((chunks,)),
            dma((2,)), dma((lines, chunks)), dma((2,)), dma((lines, chunks)),
            dma((chunks,)),
        ],
        compiler_params=pltpu.CompilerParams(
            collective_id=0, has_side_effects=True, vmem_limit_bytes=56 * 2**20),
        cost_estimate=pl.CostEstimate(
            flops=flops, bytes_accessed=20 * 2**20, transcendentals=0),
    )(features, cotangents, feedback)


def compress(matrix, old_right, replica_count):
    left = lax.dot_general(
        matrix,
        old_right,
        (((1,), (1,)), ((), ())),
        precision=lax.Precision.HIGHEST,
        preferred_element_type=jnp.float32,
    )
    left = lax.psum(left, "replica")
    basis = orthonormal(left)
    fresh = lax.dot_general(
        basis,
        matrix,
        (((0,), (0,)), ((), ())),
        precision=lax.Precision.HIGHEST,
        preferred_element_type=jnp.float32,
    )
    fresh = lax.psum(fresh, "replica")
    update = jnp.dot(basis, fresh, precision=lax.Precision.HIGHEST) / replica_count
    return (update, matrix - update, fresh)


def body(features, cotangents, feedback, factors):
    shard_count = lax.axis_size("shard")
    replica_count = lax.axis_size("replica")
    kv_width = factors.shape[3]
    grad_scale = 0.25 / math.sqrt(features.shape[0] * shard_count)
    results = []
    merged_all = merged_gradient(features, cotangents, feedback, grad_scale)
    for member in range(2):
        merged = merged_all[:, member * kv_width : (member + 1) * kv_width]
        results.append(compress(merged, factors[0, member], replica_count))
    update = jnp.concatenate([results[0][0], results[1][0]], axis=1)
    new_feedback = jnp.concatenate([results[0][1], results[1][1]], axis=1)[None]
    next_factors = jnp.stack([results[0][2], results[1][2]], axis=0)[None]
    return (update, new_feedback, next_factors)


def solution(mesh):
    return jax.shard_map(
        body,
        mesh=mesh,
        in_specs=(
            P(("groups", "shard", "replica"), None),
            P(("groups", "shard", "replica"), None),
            P("replica", ("groups", "shard"), None),
            P(("groups", "shard"), None, None, None),
        ),
        out_specs=(
            P(("groups", "shard"), None),
            P("replica", ("groups", "shard"), None),
            P(("groups", "shard"), None, None, None),
        ),
        check_vma=False,
    )
```

```python
import functools
import math

import jax
import jax.numpy as jnp
from jax import lax
from jax.experimental import pallas as pl
from jax.experimental.pallas import tpu as pltpu
from jax.sharding import PartitionSpec as P

COLS = 256
MESH = pl.DeviceIdType.MESH


def halves(value):
    high = value.astype(jnp.bfloat16)
    return high, (value - high.astype(jnp.float32)).astype(jnp.bfloat16)


def dot_t(a, b):
    return lax.dot_general(
        a, b, (((1,), (1,)), ((), ())), preferred_element_type=jnp.float32)


def inverse_factor(gram):
    rank = gram.shape[0]
    row_at = lax.broadcasted_iota(jnp.int32, (rank, rank), 0)
    col_at = lax.broadcasted_iota(jnp.int32, (rank, rank), 1)
    eye = jnp.where(row_at == col_at, 1.0, 0.0)
    table = jnp.concatenate([gram, eye], axis=1)
    index = lax.broadcasted_iota(jnp.int32, (rank, 1), 0)
    for j in range(rank):
        row = table[j : j + 1, :]
        ratio = table[:, j : j + 1] / table[j : j + 1, j : j + 1]
        table = table - jnp.where(index > j, ratio, 0.0) * row
    pivots = jnp.sum(table[:, :rank] * eye, axis=1, keepdims=True)
    return table[:, rank:] / jnp.sqrt(pivots)


def merge_kernel(
    lines, scale, by_slice, x_ref, g_ref, fb_ref, f_ref,
    out_ref, fresh_ref, b3_ref, f3_ref,
    xb, gb, up, down, acc, high, low, left, left_in, fresh, fresh_in,
    left_send, left_recv, fresh_send, fresh_recv,
    sx_loc, sg_loc, sf_loc, sx_send, sx_recv, sg_send, sg_recv,
    up_send, up_recv, down_send, down_recv, out_sem,
):
    tok = g_ref.shape[0]
    rows = xb.shape[2]
    members, rank = f_ref.shape[1], f_ref.shape[2]
    per = f_ref.shape[3] // COLS
    twin = {"replica": 1 - lax.axis_index("replica")}
    chunks = gb.shape[0]
    last = lines - 1
    me = lax.axis_index("shard")
    z = me // 2
    y = me % 2
    mate = {"shard": me + 1 - 2 * y}
    above = {"shard": jnp.minimum(me + 2, 2 * lines - 2 + y)}
    below = {"shard": jnp.maximum(me - 2, y)}
    lower = z <= last - z
    edge = jnp.minimum(z, last - z)

    def x_part(block):
        if by_slice:
            return x_ref.at[:, pl.ds(pl.multiple_of(block * rows, rows), rows)]
        return x_ref.at[block]

    def g_part(c):
        return g_ref.at[:, pl.ds(pl.multiple_of(c * COLS, COLS), COLS)]

    def x_local(d):
        return pltpu.make_async_copy(
            x_part(2 * d + y), xb.at[d, pl.ds(0, tok)], sx_loc.at[d])

    def x_remote(d):
        return pltpu.make_async_remote_copy(
            src_ref=x_part(2 * d + 1 - y), dst_ref=xb.at[d, pl.ds(tok, tok)],
            send_sem=sx_send.at[d], recv_sem=sx_recv.at[d],
            device_id=mate, device_id_type=MESH)

    def g_local(c):
        return pltpu.make_async_copy(g_part(c), gb.at[c, pl.ds(0, tok)], sg_loc.at[c])

    def g_remote(c):
        return pltpu.make_async_remote_copy(
            src_ref=g_part(c), dst_ref=gb.at[c, pl.ds(tok, tok)],
            send_sem=sg_send.at[c], recv_sem=sg_recv.at[c],
            device_id=mate, device_id_type=MESH)

    def hop(slots, send, recv, d, c, i, target):
        return pltpu.make_async_remote_copy(
            src_ref=slots.at[d, c], dst_ref=slots.at[d, c],
            send_sem=send.at[i % 2], recv_sem=recv.at[d, c],
            device_id=target, device_id_type=MESH)

    def up_hop(i):
        return hop(up, up_send, up_recv, last - i // chunks, i % chunks, i, above)

    def down_hop(i):
        return hop(down, down_send, down_recv, i // chunks, i % chunks, i, below)

    fb_copy = pltpu.make_async_copy(fb_ref.at[0], acc, sf_loc)

    barrier = pltpu.get_barrier_semaphore()
    pl.semaphore_signal(barrier, inc=1, device_id=mate, device_id_type=MESH)
    pl.semaphore_signal(barrier, inc=1, device_id=twin, device_id_type=MESH)

    @pl.when(z < last)
    def _():
        pl.semaphore_signal(barrier, inc=1, device_id=above, device_id_type=MESH)

    @pl.when(z > 0)
    def _():
        pl.semaphore_signal(barrier, inc=1, device_id=below, device_id_type=MESH)

    pl.semaphore_wait(
        barrier, 2 + jnp.where(z < last, 1, 0) + jnp.where(z > 0, 1, 0))

    def start_x(d):
        x_remote(d).start()
        x_local(d).start()

    def start_g(c):
        g_remote(c).start()
        g_local(c).start()

    first = jnp.where(lower, last, 0)
    second = jnp.where(lower, 0, last)
    start_x(first)
    start_g(0)

    @pl.when(edge > 0)
    def _():
        start_x(second)

    @pl.loop(1, chunks)
    def _(c):
        start_g(c)

    @pl.loop(1, last)
    def _(k):
        @pl.when(last - k > z)
        def _():
            start_x(last - k)

        @pl.when(k < z)
        def _():
            start_x(k)

    start_x(z)
    fb_copy.start()

    def wait_x(d):
        x_local(d).wait()
        x_remote(d).wait()

    def term(d, c):
        return lax.dot_general(
            xb[d], gb[c], (((0,), (0,)), ((), ())),
            preferred_element_type=jnp.float32) * scale

    def relay(slots, make, sends, i, d, c, inner):
        @pl.when(c == 0)
        def _():
            wait_x(d)

        value = term(d, c)

        @pl.when(i >= 2)
        def _():
            make(i - 2).wait_send()

        @pl.when(inner)
        def _():
            make(i).wait_recv()
            slots[d, c] = (value + slots[d, c].astype(jnp.float32)).astype(slots.dtype)

        @pl.when(jnp.logical_not(inner))
        def _():
            slots[d, c] = value.astype(slots.dtype)

        make(i).start()

    @pl.loop(edge, last * chunks + last)
    def _(t):
        @pl.when(t - edge < chunks)
        def _():
            g_local(t - edge).wait()
            g_remote(t - edge).wait()

        i = t - z

        @pl.when(jnp.logical_and(i >= 0, i < (last - z) * chunks))
        def _():
            relay(up, up_hop, up_send, i, last - i // chunks, i % chunks, z > 0)

        j = t - (last - z)

        @pl.when(jnp.logical_and(j >= 0, j < z * chunks))
        def _():
            relay(down, down_hop, down_send, j, j // chunks, j % chunks, z < last)

    wait_x(z)
    fb_copy.wait()
    left[...] = jnp.zeros_like(left)

    def out_copy(c):
        view = pl.ds(pl.multiple_of(c * COLS, COLS), COLS)
        return pltpu.make_async_copy(
            acc.at[:, view], out_ref.at[:, view], out_sem.at[c])

    @pl.loop(0, chunks)
    def _(c):
        view = pl.ds(pl.multiple_of(c * COLS, COLS), COLS)
        acc[:, view] += term(z, c)

        @pl.when(z > 0)
        def _():
            up_hop((last - z) * chunks + c).wait_recv()
            acc[:, view] += up[z, c].astype(jnp.float32)

        @pl.when(z < last)
        def _():
            down_hop(z * chunks + c).wait_recv()
            acc[:, view] += down[z, c].astype(jnp.float32)

        out_copy(c).start()
        hi, lo = halves(acc[:, view])
        high[c] = hi
        low[c] = lo
        member = c // per
        part = f_ref[0, member, :, pl.ds(pl.multiple_of(c % per * COLS, COLS), COLS)]
        wide = jnp.concatenate(
            [jnp.where(member == m, part, 0.0) for m in range(members)], axis=0)
        f_hi, f_lo = halves(wide)
        left[...] += dot_t(hi, f_hi) + dot_t(hi, f_lo) + dot_t(lo, f_hi)

    left_copy = pltpu.make_async_remote_copy(
        src_ref=left, dst_ref=left_in, send_sem=left_send, recv_sem=left_recv,
        device_id=twin, device_id_type=MESH)
    left_copy.start()
    left_copy.wait()
    total = left[...] + left_in[...]
    gram = lax.dot_general(
        total, total, (((0,), (0,)), ((), ())),
        precision=lax.Precision.HIGHEST, preferred_element_type=jnp.float32)
    empty = jnp.zeros((rank, rank), jnp.float32)
    inverse = jnp.concatenate([
        jnp.concatenate([
            inverse_factor(gram[m * rank : (m + 1) * rank, m * rank : (m + 1) * rank])
            if m == n else empty for n in range(members)], axis=1)
        for m in range(members)], axis=0)
    basis = lax.dot_general(
        total, inverse, (((1,), (1,)), ((), ())),
        precision=lax.Precision.HIGHEST, preferred_element_type=jnp.float32)
    b_hi, b_lo = halves(jnp.swapaxes(basis, 0, 1))
    for m in range(members):
        span = slice(m * rank, (m + 1) * rank)
        b3_ref[m] = jnp.concatenate([b_hi[span], b_hi[span], b_lo[span]], axis=0)

    def fresh_copy(c):
        return pltpu.make_async_remote_copy(
            src_ref=fresh.at[c], dst_ref=fresh_in.at[c],
            send_sem=fresh_send.at[c], recv_sem=fresh_recv.at[c],
            device_id=twin, device_id_type=MESH)

    @pl.loop(0, chunks)
    def _(c):
        both = b3_ref[c // per]
        top = jnp.dot(both[rank:], high[c], preferred_element_type=jnp.float32)
        rest = jnp.dot(both[:rank], low[c], preferred_element_type=jnp.float32)
        fresh[c] = top[:rank] + top[rank:] + rest
        fresh_copy(c).start()

    for c in range(chunks):
        fresh_copy(c).wait()
        view = slice(c % per * COLS, (c % per + 1) * COLS)
        whole = fresh[c] + fresh_in[c]
        fresh_ref[0, c // per, :, view] = whole
        w_hi, w_lo = halves(whole)
        f3_ref[c // per, :, view] = jnp.concatenate([w_hi, w_lo, w_hi], axis=0)

    @pl.loop(0, 2)
    def _(k):
        @pl.when(z < last)
        def _():
            up_hop((last - z) * chunks - 2 + k).wait_send()

        @pl.when(z > 0)
        def _():
            down_hop(z * chunks - 2 + k).wait_send()

    @pl.loop(0, chunks)
    def _(c):
        out_copy(c).wait()


def compress(features, cotangents, feedback, factors, scale):
    shard_count = lax.axis_size("shard")
    lines = shard_count // 2
    tok, width = cotangents.shape
    rows = features.shape[1] // shard_count
    members, rank, kv_width = factors.shape[1:]
    chunks = width // COLS
    by_slice = rows % 128 == 0
    if not by_slice:
        features = features.reshape(tok, shard_count, rows).transpose(1, 0, 2)
    dma = pltpu.SemaphoreType.DMA
    bf16, f32 = jnp.bfloat16, jnp.float32
    flops = 2 * tok * rows * shard_count * width
    vmem = pl.BlockSpec(memory_space=pltpu.VMEM)
    anywhere = pl.BlockSpec(memory_space=pl.ANY)
    return pl.pallas_call(
        functools.partial(merge_kernel, lines, scale, by_slice),
        out_shape=[
            jax.ShapeDtypeStruct((rows, width), f32),
            jax.ShapeDtypeStruct(factors.shape, f32),
            jax.ShapeDtypeStruct((members, 3 * rank, rows), bf16),
            jax.ShapeDtypeStruct((members, 3 * rank, kv_width), bf16),
        ],
        in_specs=[anywhere] * 3 + [vmem],
        out_specs=[anywhere, vmem, vmem, vmem],
        scratch_shapes=[
            pltpu.VMEM((lines, 2 * tok, rows), bf16),
            pltpu.VMEM((chunks, 2 * tok, COLS), bf16),
            pltpu.VMEM((lines, chunks, rows, COLS), bf16),
            pltpu.VMEM((lines, chunks, rows, COLS), bf16),
            pltpu.VMEM((rows, width), f32),
            pltpu.VMEM((chunks, rows, COLS), bf16),
            pltpu.VMEM((chunks, rows, COLS), bf16),
            pltpu.VMEM((rows, members * rank), f32),
            pltpu.VMEM((rows, members * rank), f32),
            pltpu.VMEM((chunks, rank, COLS), f32),
            pltpu.VMEM((chunks, rank, COLS), f32),
            dma, dma, dma((chunks,)), dma((chunks,)),
            dma((lines,)), dma((chunks,)), dma,
            dma((lines,)), dma((lines,)), dma((chunks,)), dma((chunks,)),
            dma((2,)), dma((lines, chunks)), dma((2,)), dma((lines, chunks)),
            dma((chunks,)),
        ],
        compiler_params=pltpu.CompilerParams(
            collective_id=0, has_side_effects=True, vmem_limit_bytes=58 * 2**20),
        cost_estimate=pl.CostEstimate(
            flops=flops, bytes_accessed=20 * 2**20, transcendentals=0),
    )(features, cotangents, feedback, factors)


def spread_kernel(replica_count, b3_ref, f3_ref, merged_ref, update_ref, rest_ref):
    product = lax.dot_general(
        b3_ref[0], f3_ref[0], (((0,), (0,)), ((), ())),
        preferred_element_type=jnp.float32)
    update = product / replica_count
    update_ref[...] = update
    rest_ref[0] = merged_ref[...] - update


def spread(b3, f3, merged, replica_count):
    rows, width = merged.shape
    per = f3.shape[2] // COLS
    cols = pl.BlockSpec((rows, COLS), lambda c: (0, c))
    return pl.pallas_call(
        functools.partial(spread_kernel, replica_count),
        grid=(width // COLS,),
        out_shape=[
            jax.ShapeDtypeStruct((rows, width), jnp.float32),
            jax.ShapeDtypeStruct((1, rows, width), jnp.float32),
        ],
        in_specs=[
            pl.BlockSpec((1,) + b3.shape[1:], lambda c: (c // per, 0, 0)),
            pl.BlockSpec((1, f3.shape[1], COLS), lambda c: (c // per, 0, c % per)),
            cols,
        ],
        out_specs=[cols, pl.BlockSpec((1, rows, COLS), lambda c: (0, 0, c))],
        compiler_params=pltpu.CompilerParams(vmem_limit_bytes=32 * 2**20),
    )(b3, f3, merged)


def body(features, cotangents, feedback, factors):
    grad_scale = 0.25 / math.sqrt(features.shape[0] * lax.axis_size("shard"))
    merged, next_factors, b3, f3 = compress(
        features, cotangents, feedback, factors, grad_scale)
    update, new_feedback = spread(b3, f3, merged, lax.axis_size("replica"))
    return (update, new_feedback, next_factors)


def solution(mesh):
    return jax.shard_map(
        body,
        mesh=mesh,
        in_specs=(
            P(("groups", "shard", "replica"), None),
            P(("groups", "shard", "replica"), None),
            P("replica", ("groups", "shard"), None),
            P(("groups", "shard"), None, None, None),
        ),
        out_specs=(
            P(("groups", "shard"), None),
            P("replica", ("groups", "shard"), None),
            P(("groups", "shard"), None, None, None),
        ),
        check_vma=False,
    )
```

```python
import functools
import math

import jax
import jax.numpy as jnp
from jax import lax
from jax.experimental import pallas as pl
from jax.experimental.pallas import tpu as pltpu
from jax.sharding import PartitionSpec as P

COLS = 128
WIDE = 256
DEPTH = 4
MESH = pl.DeviceIdType.MESH


def halves(value):
    high = value.astype(jnp.bfloat16)
    return high, (value - high.astype(jnp.float32)).astype(jnp.bfloat16)


def dot_t(a, b):
    return lax.dot_general(
        a, b, (((1,), (1,)), ((), ())), preferred_element_type=jnp.float32)


def inverse_factor(gram):
    rank = gram.shape[0]
    row_at = lax.broadcasted_iota(jnp.int32, (rank, rank), 0)
    col_at = lax.broadcasted_iota(jnp.int32, (rank, rank), 1)
    eye = jnp.where(row_at == col_at, 1.0, 0.0)
    table = jnp.concatenate([gram, eye], axis=1)
    index = lax.broadcasted_iota(jnp.int32, (rank, 1), 0)
    for j in range(rank):
        row = table[j : j + 1, :]
        ratio = table[:, j : j + 1] / table[j : j + 1, j : j + 1]
        table = table - jnp.where(index > j, ratio, 0.0) * row
    pivots = jnp.sum(table[:, :rank] * eye, axis=1, keepdims=True)
    return table[:, rank:] / jnp.sqrt(pivots)


def merge_kernel(
    lines, scale, by_slice, x_ref, g_ref, fb_ref, f_ref,
    out_ref, fresh_ref, b3_ref,
    xb, xt, gb, up, down, acc, high, low, left, left_in, fresh, fresh_in,
    left_send, left_recv, fresh_send, fresh_recv,
    sx_loc, sg_loc, sf_loc, sx_send, sx_recv, sg_send, sg_recv,
    up_send, up_recv, down_send, down_recv, out_sem,
):
    tok = g_ref.shape[0]
    rows = xb.shape[2]
    members, rank = f_ref.shape[1], f_ref.shape[2]
    per = f_ref.shape[3] // COLS
    twin = {"replica": 1 - lax.axis_index("replica")}
    chunks = gb.shape[0]
    last = lines - 1
    me = lax.axis_index("shard")
    z = me // 2
    y = me % 2
    mate = {"shard": me + 1 - 2 * y}
    above = {"shard": jnp.minimum(me + 2, 2 * lines - 2 + y)}
    below = {"shard": jnp.maximum(me - 2, y)}
    lower = z <= last - z
    edge = jnp.minimum(z, last - z)

    def x_part(block):
        if by_slice:
            return x_ref.at[:, pl.ds(pl.multiple_of(block * rows, rows), rows)]
        return x_ref.at[block]

    def g_part(c):
        return g_ref.at[:, pl.ds(pl.multiple_of(c * COLS, COLS), COLS)]

    def x_local(d):
        return pltpu.make_async_copy(
            x_part(2 * d + y), xb.at[d, pl.ds(0, tok)], sx_loc.at[d])

    def x_remote(d):
        return pltpu.make_async_remote_copy(
            src_ref=x_part(2 * d + 1 - y), dst_ref=xb.at[d, pl.ds(tok, tok)],
            send_sem=sx_send.at[d], recv_sem=sx_recv.at[d],
            device_id=mate, device_id_type=MESH)

    def g_local(c):
        return pltpu.make_async_copy(g_part(c), gb.at[c, pl.ds(0, tok)], sg_loc.at[c])

    def g_remote(c):
        return pltpu.make_async_remote_copy(
            src_ref=g_part(c), dst_ref=gb.at[c, pl.ds(tok, tok)],
            send_sem=sg_send.at[c], recv_sem=sg_recv.at[c],
            device_id=mate, device_id_type=MESH)

    def hop(slots, send, recv, d, c, i, target):
        return pltpu.make_async_remote_copy(
            src_ref=slots.at[d, c], dst_ref=slots.at[d, c],
            send_sem=send.at[i % DEPTH], recv_sem=recv.at[d, c],
            device_id=target, device_id_type=MESH)

    def up_hop(i):
        return hop(up, up_send, up_recv, last - i // chunks, i % chunks, i, above)

    def down_hop(i):
        return hop(down, down_send, down_recv, i // chunks, i % chunks, i, below)

    fb_copy = pltpu.make_async_copy(fb_ref.at[0], acc, sf_loc)

    barrier = pltpu.get_barrier_semaphore()
    pl.semaphore_signal(barrier, inc=1, device_id=mate, device_id_type=MESH)
    pl.semaphore_signal(barrier, inc=1, device_id=twin, device_id_type=MESH)

    @pl.when(z < last)
    def _():
        pl.semaphore_signal(barrier, inc=1, device_id=above, device_id_type=MESH)

    @pl.when(z > 0)
    def _():
        pl.semaphore_signal(barrier, inc=1, device_id=below, device_id_type=MESH)

    pl.semaphore_wait(
        barrier, 2 + jnp.where(z < last, 1, 0) + jnp.where(z > 0, 1, 0))

    def start_x(d):
        x_remote(d).start()
        x_local(d).start()

    def start_g(c):
        g_remote(c).start()
        g_local(c).start()

    first = jnp.where(lower, last, 0)
    second = jnp.where(lower, 0, last)
    start_x(first)
    start_g(0)

    @pl.when(edge > 0)
    def _():
        start_x(second)

    @pl.loop(1, chunks)
    def _(c):
        start_g(c)

    @pl.loop(1, last)
    def _(k):
        @pl.when(last - k > z)
        def _():
            start_x(last - k)

        @pl.when(k < z)
        def _():
            start_x(k)

    start_x(z)
    fb_copy.start()

    def wait_x(d):
        x_local(d).wait()
        x_remote(d).wait()
        xt[d] = jnp.swapaxes(xb[d], 0, 1)

    def term(d, c):
        return jnp.dot(xt[d], gb[c], preferred_element_type=jnp.float32) * scale

    def relay(slots, make, sends, i, d, c, inner):
        @pl.when(c == 0)
        def _():
            wait_x(d)

        value = term(d, c)

        @pl.when(i >= DEPTH)
        def _():
            make(i - DEPTH).wait_send()

        @pl.when(inner)
        def _():
            make(i).wait_recv()
            slots[d, c] = (value + slots[d, c].astype(jnp.float32)).astype(slots.dtype)

        @pl.when(jnp.logical_not(inner))
        def _():
            slots[d, c] = value.astype(slots.dtype)

        make(i).start()

    @pl.loop(edge, last * chunks + last)
    def _(t):
        @pl.when(t - edge < chunks)
        def _():
            g_local(t - edge).wait()
            g_remote(t - edge).wait()

        i = t - z

        @pl.when(jnp.logical_and(i >= 0, i < (last - z) * chunks))
        def _():
            relay(up, up_hop, up_send, i, last - i // chunks, i % chunks, z > 0)

        j = t - (last - z)

        @pl.when(jnp.logical_and(j >= 0, j < z * chunks))
        def _():
            relay(down, down_hop, down_send, j, j // chunks, j % chunks, z < last)

    wait_x(z)
    fb_copy.wait()
    left[...] = jnp.zeros_like(left)

    def out_copy(c):
        view = pl.ds(pl.multiple_of(c * COLS, COLS), COLS)
        return pltpu.make_async_copy(
            acc.at[:, view], out_ref.at[:, view], out_sem.at[c])

    @pl.loop(0, chunks)
    def _(c):
        view = pl.ds(pl.multiple_of(c * COLS, COLS), COLS)
        acc[:, view] += term(z, c)

        @pl.when(z > 0)
        def _():
            up_hop((last - z) * chunks + c).wait_recv()
            acc[:, view] += up[z, c].astype(jnp.float32)

        @pl.when(z < last)
        def _():
            down_hop(z * chunks + c).wait_recv()
            acc[:, view] += down[z, c].astype(jnp.float32)

        out_copy(c).start()
        hi, lo = halves(acc[:, view])
        lanes = pl.ds(pl.multiple_of(c * COLS % WIDE, COLS), COLS)
        high[c * COLS // WIDE, :, lanes] = hi
        low[c * COLS // WIDE, :, lanes] = lo
        member = c // per
        part = f_ref[0, member, :, pl.ds(pl.multiple_of(c % per * COLS, COLS), COLS)]
        wide = jnp.concatenate(
            [jnp.where(member == m, part, 0.0) for m in range(members)], axis=0)
        f_hi, f_lo = halves(wide)
        left[...] += dot_t(hi, f_hi) + dot_t(hi, f_lo) + dot_t(lo, f_hi)

    left_copy = pltpu.make_async_remote_copy(
        src_ref=left, dst_ref=left_in, send_sem=left_send, recv_sem=left_recv,
        device_id=twin, device_id_type=MESH)
    left_copy.start()
    left_copy.wait()
    total = left[...] + left_in[...]
    gram = lax.dot_general(
        total, total, (((0,), (0,)), ((), ())),
        precision=lax.Precision.HIGHEST, preferred_element_type=jnp.float32)
    empty = jnp.zeros((rank, rank), jnp.float32)
    inverse = jnp.concatenate([
        jnp.concatenate([
            inverse_factor(gram[m * rank : (m + 1) * rank, m * rank : (m + 1) * rank])
            if m == n else empty for n in range(members)], axis=1)
        for m in range(members)], axis=0)
    basis = lax.dot_general(
        total, inverse, (((1,), (1,)), ((), ())),
        precision=lax.Precision.HIGHEST, preferred_element_type=jnp.float32)
    b_hi, b_lo = halves(jnp.swapaxes(basis, 0, 1))
    for m in range(members):
        span = slice(m * rank, (m + 1) * rank)
        b3_ref[m] = jnp.concatenate([b_hi[span], b_hi[span], b_lo[span]], axis=0)

    def fresh_copy(c):
        return pltpu.make_async_remote_copy(
            src_ref=fresh.at[c], dst_ref=fresh_in.at[c],
            send_sem=fresh_send.at[c], recv_sem=fresh_recv.at[c],
            device_id=twin, device_id_type=MESH)

    wide_count = high.shape[0]
    wide_per = wide_count // members

    @pl.loop(0, wide_count)
    def _(c):
        both = b3_ref[c // wide_per]
        top = jnp.dot(both[rank:], high[c], preferred_element_type=jnp.float32)
        rest = jnp.dot(both[:rank], low[c], preferred_element_type=jnp.float32)
        fresh[c] = top[:rank] + top[rank:] + rest
        fresh_copy(c).start()

    for c in range(wide_count):
        fresh_copy(c).wait()
        view = slice(c % wide_per * WIDE, (c % wide_per + 1) * WIDE)
        fresh_ref[0, c // wide_per, :, view] = fresh[c] + fresh_in[c]

    @pl.loop(0, DEPTH)
    def _(k):
        @pl.when(z < last)
        def _():
            up_hop((last - z) * chunks - DEPTH + k).wait_send()

        @pl.when(z > 0)
        def _():
            down_hop(z * chunks - DEPTH + k).wait_send()

    @pl.loop(0, chunks)
    def _(c):
        out_copy(c).wait()


def compress(features, cotangents, feedback, factors, scale):
    shard_count = lax.axis_size("shard")
    lines = shard_count // 2
    tok, width = cotangents.shape
    rows = features.shape[1] // shard_count
    members, rank = factors.shape[1:3]
    chunks = width // COLS
    by_slice = rows % 128 == 0
    if not by_slice:
        features = features.reshape(tok, shard_count, rows).transpose(1, 0, 2)
    dma = pltpu.SemaphoreType.DMA
    bf16, f32 = jnp.bfloat16, jnp.float32
    flops = 2 * tok * rows * shard_count * width
    vmem = pl.BlockSpec(memory_space=pltpu.VMEM)
    anywhere = pl.BlockSpec(memory_space=pl.ANY)
    return pl.pallas_call(
        functools.partial(merge_kernel, lines, scale, by_slice),
        out_shape=[
            jax.ShapeDtypeStruct((rows, width), f32),
            jax.ShapeDtypeStruct(factors.shape, f32),
            jax.ShapeDtypeStruct((members, 3 * rank, rows), bf16),
        ],
        in_specs=[anywhere] * 3 + [vmem],
        out_specs=[anywhere, vmem, vmem],
        scratch_shapes=[
            pltpu.VMEM((lines, 2 * tok, rows), bf16),
            pltpu.VMEM((lines, rows, 2 * tok), bf16),
            pltpu.VMEM((chunks, 2 * tok, COLS), bf16),
            pltpu.VMEM((lines, chunks, rows, COLS), bf16),
            pltpu.VMEM((lines, chunks, rows, COLS), bf16),
            pltpu.VMEM((rows, width), f32),
            pltpu.VMEM((width // WIDE, rows, WIDE), bf16),
            pltpu.VMEM((width // WIDE, rows, WIDE), bf16),
            pltpu.VMEM((rows, members * rank), f32),
            pltpu.VMEM((rows, members * rank), f32),
            pltpu.VMEM((width // WIDE, rank, WIDE), f32),
            pltpu.VMEM((width // WIDE, rank, WIDE), f32),
            dma, dma, dma((width // WIDE,)), dma((width // WIDE,)),
            dma((lines,)), dma((chunks,)), dma,
            dma((lines,)), dma((lines,)), dma((chunks,)), dma((chunks,)),
            dma((DEPTH,)), dma((lines, chunks)), dma((DEPTH,)), dma((lines, chunks)),
            dma((chunks,)),
        ],
        compiler_params=pltpu.CompilerParams(
            collective_id=0, has_side_effects=True, vmem_limit_bytes=58 * 2**20),
        cost_estimate=pl.CostEstimate(
            flops=flops, bytes_accessed=20 * 2**20, transcendentals=0),
    )(features, cotangents, feedback, factors)


def spread_kernel(replica_count, b3_ref, fresh_ref, merged_ref, update_ref, rest_ref, next_ref):
    next_ref[...] = fresh_ref[...]
    width = fresh_ref.shape[3]
    for m in range(fresh_ref.shape[1]):
        hi, lo = halves(fresh_ref[0, m])
        product = lax.dot_general(
            b3_ref[m], jnp.concatenate([hi, lo, hi], axis=0), (((0,), (0,)), ((), ())),
            preferred_element_type=jnp.float32)
        update = product / replica_count
        view = slice(m * width, (m + 1) * width)
        update_ref[:, view] = update
        rest_ref[0, :, view] = merged_ref[:, view] - update


def spread(b3, fresh, merged, replica_count):
    rows, width = merged.shape
    strip = 128 if rows % 128 == 0 else rows
    strips = pl.BlockSpec((strip, width), lambda i: (i, 0))
    whole = pl.BlockSpec(fresh.shape, lambda i: (0, 0, 0, 0))
    return pl.pallas_call(
        functools.partial(spread_kernel, replica_count),
        grid=(rows // strip,),
        out_shape=[
            jax.ShapeDtypeStruct((rows, width), jnp.float32),
            jax.ShapeDtypeStruct((1, rows, width), jnp.float32),
            jax.ShapeDtypeStruct(fresh.shape, jnp.float32),
        ],
        in_specs=[
            pl.BlockSpec(b3.shape[:2] + (strip,), lambda i: (0, 0, i)),
            whole,
            strips,
        ],
        out_specs=[strips, pl.BlockSpec((1, strip, width), lambda i: (0, i, 0)), whole],
        compiler_params=pltpu.CompilerParams(vmem_limit_bytes=58 * 2**20),
    )(b3, fresh, merged)


def body(features, cotangents, feedback, factors):
    grad_scale = 0.25 / math.sqrt(features.shape[0] * lax.axis_size("shard"))
    merged, fresh, b3 = compress(
        features, cotangents, feedback, factors, grad_scale)
    update, new_feedback, next_factors = spread(
        b3, fresh, merged, lax.axis_size("replica"))
    return (update, new_feedback, next_factors)


def solution(mesh):
    return jax.shard_map(
        body,
        mesh=mesh,
        in_specs=(
            P(("groups", "shard", "replica"), None),
            P(("groups", "shard", "replica"), None),
            P("replica", ("groups", "shard"), None),
            P(("groups", "shard"), None, None, None),
        ),
        out_specs=(
            P(("groups", "shard"), None),
            P("replica", ("groups", "shard"), None),
            P(("groups", "shard"), None, None, None),
        ),
        check_vma=False,
    )
```

```python
import functools
import math

import jax
import jax.numpy as jnp
from jax import lax
from jax.experimental import pallas as pl
from jax.experimental.pallas import tpu as pltpu
from jax.sharding import PartitionSpec as P

COLS = 128
WIDE = 256
DEPTH = 4
MESH = pl.DeviceIdType.MESH


def halves(value):
    high = value.astype(jnp.bfloat16)
    return high, (value - high.astype(jnp.float32)).astype(jnp.bfloat16)


def dot_t(a, b):
    return lax.dot_general(
        a, b, (((1,), (1,)), ((), ())), preferred_element_type=jnp.float32)


def inverse_factor(gram):
    rank = gram.shape[0]
    row_at = lax.broadcasted_iota(jnp.int32, (rank, rank), 0)
    col_at = lax.broadcasted_iota(jnp.int32, (rank, rank), 1)
    eye = jnp.where(row_at == col_at, 1.0, 0.0)
    table = jnp.concatenate([gram, eye], axis=1)
    index = lax.broadcasted_iota(jnp.int32, (rank, 1), 0)
    for j in range(rank):
        row = table[j : j + 1, :]
        ratio = table[:, j : j + 1] / table[j : j + 1, j : j + 1]
        table = table - jnp.where(index > j, ratio, 0.0) * row
    pivots = jnp.sum(table[:, :rank] * eye, axis=1, keepdims=True)
    return table[:, rank:] / jnp.sqrt(pivots)


def merge_kernel(
    lines, scale, by_slice, x_ref, g_ref, fb_ref, f_ref,
    out_ref, fresh_ref, b3_ref,
    xb, xt, gb, up, down, acc, high, low, left, left_in, fresh, fresh_in,
    left_send, left_recv, fresh_send, fresh_recv,
    sx_loc, sg_loc, sf_loc, sx_send, sx_recv, sg_send, sg_recv,
    up_send, up_recv, down_send, down_recv, out_sem,
):
    tok = g_ref.shape[0]
    rows = xb.shape[2]
    members, rank = f_ref.shape[1], f_ref.shape[2]
    per = f_ref.shape[3] // COLS
    twin = {"replica": 1 - lax.axis_index("replica")}
    chunks = gb.shape[0]
    last = lines - 1
    me = lax.axis_index("shard")
    z = me // 2
    y = me % 2
    mate = {"shard": me + 1 - 2 * y}
    above = {"shard": jnp.minimum(me + 2, 2 * lines - 2 + y)}
    below = {"shard": jnp.maximum(me - 2, y)}
    lower = z <= last - z
    edge = jnp.minimum(z, last - z)

    def x_part(block):
        if by_slice:
            return x_ref.at[:, pl.ds(pl.multiple_of(block * rows, rows), rows)]
        return x_ref.at[block]

    def g_part(c):
        return g_ref.at[:, pl.ds(pl.multiple_of(c * COLS, COLS), COLS)]

    def x_local(d):
        return pltpu.make_async_copy(
            x_part(2 * d + y), xb.at[d, pl.ds(0, tok)], sx_loc.at[d])

    def x_remote(d):
        return pltpu.make_async_remote_copy(
            src_ref=x_part(2 * d + 1 - y), dst_ref=xb.at[d, pl.ds(tok, tok)],
            send_sem=sx_send.at[d], recv_sem=sx_recv.at[d],
            device_id=mate, device_id_type=MESH)

    def g_local(c):
        return pltpu.make_async_copy(g_part(c), gb.at[c, pl.ds(0, tok)], sg_loc.at[c])

    def g_remote(c):
        return pltpu.make_async_remote_copy(
            src_ref=g_part(c), dst_ref=gb.at[c, pl.ds(tok, tok)],
            send_sem=sg_send.at[c], recv_sem=sg_recv.at[c],
            device_id=mate, device_id_type=MESH)

    def hop(slots, send, recv, d, c, i, target):
        return pltpu.make_async_remote_copy(
            src_ref=slots.at[d, c], dst_ref=slots.at[d, c],
            send_sem=send.at[i % DEPTH], recv_sem=recv.at[d, c],
            device_id=target, device_id_type=MESH)

    def up_hop(i):
        return hop(up, up_send, up_recv, last - i // chunks, i % chunks, i, above)

    def down_hop(i):
        return hop(down, down_send, down_recv, i // chunks, i % chunks, i, below)

    fb_copy = pltpu.make_async_copy(fb_ref.at[0], acc, sf_loc)

    barrier = pltpu.get_barrier_semaphore()
    pl.semaphore_signal(barrier, inc=1, device_id=mate, device_id_type=MESH)
    pl.semaphore_signal(barrier, inc=1, device_id=twin, device_id_type=MESH)

    @pl.when(z < last)
    def _():
        pl.semaphore_signal(barrier, inc=1, device_id=above, device_id_type=MESH)

    @pl.when(z > 0)
    def _():
        pl.semaphore_signal(barrier, inc=1, device_id=below, device_id_type=MESH)

    pl.semaphore_wait(
        barrier, 2 + jnp.where(z < last, 1, 0) + jnp.where(z > 0, 1, 0))

    def start_x(d):
        x_remote(d).start()
        x_local(d).start()

    def start_g(c):
        g_remote(c).start()
        g_local(c).start()

    first = jnp.where(lower, last, 0)
    second = jnp.where(lower, 0, last)
    start_x(first)
    start_g(0)

    @pl.when(edge > 0)
    def _():
        start_x(second)

    @pl.loop(1, chunks)
    def _(c):
        start_g(c)

    @pl.loop(1, last)
    def _(k):
        @pl.when(last - k > z)
        def _():
            start_x(last - k)

        @pl.when(k < z)
        def _():
            start_x(k)

    start_x(z)
    fb_copy.start()

    def wait_x(d):
        x_local(d).wait()
        x_remote(d).wait()
        xt[d] = jnp.swapaxes(xb[d], 0, 1)

    def term(d, c):
        return jnp.dot(xt[d], gb[c], preferred_element_type=jnp.float32) * scale

    def relay(slots, make, sends, i, d, c, inner):
        @pl.when(c == 0)
        def _():
            wait_x(d)

        value = term(d, c)

        @pl.when(i >= DEPTH)
        def _():
            make(i - DEPTH).wait_send()

        @pl.when(inner)
        def _():
            make(i).wait_recv()
            slots[d, c] = (value + slots[d, c].astype(jnp.float32)).astype(slots.dtype)

        @pl.when(jnp.logical_not(inner))
        def _():
            slots[d, c] = value.astype(slots.dtype)

        make(i).start()

    left[...] = jnp.zeros_like(left)

    def out_copy(c):
        view = pl.ds(pl.multiple_of(c * COLS, COLS), COLS)
        return pltpu.make_async_copy(
            acc.at[:, view], out_ref.at[:, view], out_sem.at[c])

    def settle(c):
        @pl.when(c == 0)
        def _():
            wait_x(z)
            fb_copy.wait()

        view = pl.ds(pl.multiple_of(c * COLS, COLS), COLS)
        acc[:, view] += term(z, c)

        @pl.when(z > 0)
        def _():
            up_hop((last - z) * chunks + c).wait_recv()
            acc[:, view] += up[z, c].astype(jnp.float32)

        @pl.when(z < last)
        def _():
            down_hop(z * chunks + c).wait_recv()
            acc[:, view] += down[z, c].astype(jnp.float32)

        out_copy(c).start()
        hi, lo = halves(acc[:, view])
        lanes = pl.ds(pl.multiple_of(c * COLS % WIDE, COLS), COLS)
        high[c * COLS // WIDE, :, lanes] = hi
        low[c * COLS // WIDE, :, lanes] = lo
        member = c // per
        part = f_ref[0, member, :, pl.ds(pl.multiple_of(c % per * COLS, COLS), COLS)]
        wide = jnp.concatenate(
            [jnp.where(member == m, part, 0.0) for m in range(members)], axis=0)
        f_hi, f_lo = halves(wide)
        left[...] += dot_t(hi, f_hi) + dot_t(hi, f_lo) + dot_t(lo, f_hi)

    settle_at = jnp.where(
        edge > 0,
        jnp.maximum((last - z) * chunks + z, z * chunks + last - z),
        (last - 1) * chunks)

    @pl.loop(edge, last * chunks + last)
    def _(t):
        @pl.when(t - edge < chunks)
        def _():
            g_local(t - edge).wait()
            g_remote(t - edge).wait()

        i = t - z

        @pl.when(jnp.logical_and(i >= 0, i < (last - z) * chunks))
        def _():
            relay(up, up_hop, up_send, i, last - i // chunks, i % chunks, z > 0)

        j = t - (last - z)

        @pl.when(jnp.logical_and(j >= 0, j < z * chunks))
        def _():
            relay(down, down_hop, down_send, j, j // chunks, j % chunks, z < last)

        own = t - settle_at

        @pl.when(jnp.logical_and(own >= 0, own < chunks))
        def _():
            settle(own)

    left_copy = pltpu.make_async_remote_copy(
        src_ref=left, dst_ref=left_in, send_sem=left_send, recv_sem=left_recv,
        device_id=twin, device_id_type=MESH)
    left_copy.start()
    left_copy.wait()
    total = left[...] + left_in[...]
    gram = lax.dot_general(
        total, total, (((0,), (0,)), ((), ())),
        precision=lax.Precision.HIGHEST, preferred_element_type=jnp.float32)
    empty = jnp.zeros((rank, rank), jnp.float32)
    inverse = jnp.concatenate([
        jnp.concatenate([
            inverse_factor(gram[m * rank : (m + 1) * rank, m * rank : (m + 1) * rank])
            if m == n else empty for n in range(members)], axis=1)
        for m in range(members)], axis=0)
    basis = lax.dot_general(
        total, inverse, (((1,), (1,)), ((), ())),
        precision=lax.Precision.HIGHEST, preferred_element_type=jnp.float32)
    b_hi, b_lo = halves(jnp.swapaxes(basis, 0, 1))
    for m in range(members):
        span = slice(m * rank, (m + 1) * rank)
        b3_ref[m] = jnp.concatenate([b_hi[span], b_hi[span], b_lo[span]], axis=0)

    def fresh_copy(c):
        return pltpu.make_async_remote_copy(
            src_ref=fresh.at[c], dst_ref=fresh_in.at[c],
            send_sem=fresh_send.at[c], recv_sem=fresh_recv.at[c],
            device_id=twin, device_id_type=MESH)

    wide_count = high.shape[0]
    wide_per = wide_count // members

    @pl.loop(0, wide_count)
    def _(c):
        both = b3_ref[c // wide_per]
        top = jnp.dot(both[rank:], high[c], preferred_element_type=jnp.float32)
        rest = jnp.dot(both[:rank], low[c], preferred_element_type=jnp.float32)
        fresh[c] = top[:rank] + top[rank:] + rest
        fresh_copy(c).start()

    for c in range(wide_count):
        fresh_copy(c).wait()
        view = slice(c % wide_per * WIDE, (c % wide_per + 1) * WIDE)
        fresh_ref[0, c // wide_per, :, view] = fresh[c] + fresh_in[c]

    @pl.loop(0, DEPTH)
    def _(k):
        @pl.when(z < last)
        def _():
            up_hop((last - z) * chunks - DEPTH + k).wait_send()

        @pl.when(z > 0)
        def _():
            down_hop(z * chunks - DEPTH + k).wait_send()

    @pl.loop(0, chunks)
    def _(c):
        out_copy(c).wait()


def compress(features, cotangents, feedback, factors, scale):
    shard_count = lax.axis_size("shard")
    lines = shard_count // 2
    tok, width = cotangents.shape
    rows = features.shape[1] // shard_count
    members, rank = factors.shape[1:3]
    chunks = width // COLS
    by_slice = rows % 128 == 0
    if not by_slice:
        features = features.reshape(tok, shard_count, rows).transpose(1, 0, 2)
    dma = pltpu.SemaphoreType.DMA
    bf16, f32 = jnp.bfloat16, jnp.float32
    flops = 2 * tok * rows * shard_count * width
    vmem = pl.BlockSpec(memory_space=pltpu.VMEM)
    anywhere = pl.BlockSpec(memory_space=pl.ANY)
    return pl.pallas_call(
        functools.partial(merge_kernel, lines, scale, by_slice),
        out_shape=[
            jax.ShapeDtypeStruct((rows, width), f32),
            jax.ShapeDtypeStruct(factors.shape, f32),
            jax.ShapeDtypeStruct((members, 3 * rank, rows), bf16),
        ],
        in_specs=[anywhere] * 3 + [vmem],
        out_specs=[anywhere, vmem, vmem],
        scratch_shapes=[
            pltpu.VMEM((lines, 2 * tok, rows), bf16),
            pltpu.VMEM((lines, rows, 2 * tok), bf16),
            pltpu.VMEM((chunks, 2 * tok, COLS), bf16),
            pltpu.VMEM((lines, chunks, rows, COLS), bf16),
            pltpu.VMEM((lines, chunks, rows, COLS), bf16),
            pltpu.VMEM((rows, width), f32),
            pltpu.VMEM((width // WIDE, rows, WIDE), bf16),
            pltpu.VMEM((width // WIDE, rows, WIDE), bf16),
            pltpu.VMEM((rows, members * rank), f32),
            pltpu.VMEM((rows, members * rank), f32),
            pltpu.VMEM((width // WIDE, rank, WIDE), f32),
            pltpu.VMEM((width // WIDE, rank, WIDE), f32),
            dma, dma, dma((width // WIDE,)), dma((width // WIDE,)),
            dma((lines,)), dma((chunks,)), dma,
            dma((lines,)), dma((lines,)), dma((chunks,)), dma((chunks,)),
            dma((DEPTH,)), dma((lines, chunks)), dma((DEPTH,)), dma((lines, chunks)),
            dma((chunks,)),
        ],
        compiler_params=pltpu.CompilerParams(
            collective_id=0, has_side_effects=True, vmem_limit_bytes=58 * 2**20),
        cost_estimate=pl.CostEstimate(
            flops=flops, bytes_accessed=20 * 2**20, transcendentals=0),
    )(features, cotangents, feedback, factors)


def spread_kernel(replica_count, b3_ref, fresh_ref, merged_ref, update_ref, rest_ref, next_ref):
    value = fresh_ref[...]
    next_ref[...] = value
    hi, lo = halves(value[0, 0])
    product = lax.dot_general(
        b3_ref[0], jnp.concatenate([hi, lo, hi], axis=0), (((0,), (0,)), ((), ())),
        preferred_element_type=jnp.float32)
    update = product / replica_count
    update_ref[...] = update
    rest_ref[0] = merged_ref[...] - update


def spread(b3, fresh, merged, replica_count):
    rows, width = merged.shape
    members, rank, kv_width = fresh.shape[1:]
    strip = 128 if rows % 128 == 0 else rows
    strips = pl.BlockSpec((strip, kv_width), lambda m, i: (i, m))
    member = pl.BlockSpec((1, 1, rank, kv_width), lambda m, i: (0, m, 0, 0))
    return pl.pallas_call(
        functools.partial(spread_kernel, replica_count),
        grid=(members, rows // strip),
        out_shape=[
            jax.ShapeDtypeStruct((rows, width), jnp.float32),
            jax.ShapeDtypeStruct((1, rows, width), jnp.float32),
            jax.ShapeDtypeStruct(fresh.shape, jnp.float32),
        ],
        in_specs=[
            pl.BlockSpec((1, b3.shape[1], strip), lambda m, i: (m, 0, i)),
            member,
            strips,
        ],
        out_specs=[
            strips,
            pl.BlockSpec((1, strip, kv_width), lambda m, i: (0, i, m)),
            member,
        ],
        compiler_params=pltpu.CompilerParams(vmem_limit_bytes=58 * 2**20),
    )(b3, fresh, merged)


def body(features, cotangents, feedback, factors):
    grad_scale = 0.25 / math.sqrt(features.shape[0] * lax.axis_size("shard"))
    merged, fresh, b3 = compress(
        features, cotangents, feedback, factors, grad_scale)
    update, new_feedback, next_factors = spread(
        b3, fresh, merged, lax.axis_size("replica"))
    return (update, new_feedback, next_factors)


def solution(mesh):
    return jax.shard_map(
        body,
        mesh=mesh,
        in_specs=(
            P(("groups", "shard", "replica"), None),
            P(("groups", "shard", "replica"), None),
            P("replica", ("groups", "shard"), None),
            P(("groups", "shard"), None, None, None),
        ),
        out_specs=(
            P(("groups", "shard"), None),
            P("replica", ("groups", "shard"), None),
            P(("groups", "shard"), None, None, None),
        ),
        check_vma=False,
    )
```

```python
import functools
import math

import jax
import jax.numpy as jnp
from jax import lax
from jax.experimental import pallas as pl
from jax.experimental.pallas import tpu as pltpu
from jax.sharding import PartitionSpec as P

COLS = 128
WIDE = 256
DEPTH = 4
MESH = pl.DeviceIdType.MESH


def halves(value):
    high = value.astype(jnp.bfloat16)
    return high, (value - high.astype(jnp.float32)).astype(jnp.bfloat16)


def dot_t(a, b):
    return lax.dot_general(
        a, b, (((1,), (1,)), ((), ())), preferred_element_type=jnp.float32)


def inverse_factor(gram):
    rank = gram.shape[0]
    row_at = lax.broadcasted_iota(jnp.int32, (rank, rank), 0)
    col_at = lax.broadcasted_iota(jnp.int32, (rank, rank), 1)
    eye = jnp.where(row_at == col_at, 1.0, 0.0)
    table = jnp.concatenate([gram, eye], axis=1)
    index = lax.broadcasted_iota(jnp.int32, (rank, 1), 0)
    for j in range(rank):
        row = table[j : j + 1, :]
        ratio = table[:, j : j + 1] / table[j : j + 1, j : j + 1]
        table = table - jnp.where(index > j, ratio, 0.0) * row
    pivots = jnp.sum(table[:, :rank] * eye, axis=1, keepdims=True)
    return table[:, rank:] / jnp.sqrt(pivots)


def merge_kernel(
    lines, scale, by_slice, x_ref, g_ref, fb_ref, f_ref,
    out_ref, fresh_ref, b3_ref,
    xb, xt, gb, up, down, acc, high, low, left, left_in, fresh, fresh_in,
    left_send, left_recv, fresh_send, fresh_recv,
    sx_loc, sg_loc, sf_loc, sx_send, sx_recv, sg_send, sg_recv,
    up_send, up_recv, down_send, down_recv, out_sem,
):
    tok = g_ref.shape[0]
    rows = xb.shape[2]
    members, rank = f_ref.shape[1], f_ref.shape[2]
    per = f_ref.shape[3] // COLS
    twin = {"replica": 1 - lax.axis_index("replica")}
    chunks = gb.shape[0]
    last = lines - 1
    me = lax.axis_index("shard")
    z = me // 2
    y = me % 2
    mate = {"shard": me + 1 - 2 * y}
    above = {"shard": jnp.minimum(me + 2, 2 * lines - 2 + y)}
    below = {"shard": jnp.maximum(me - 2, y)}
    lower = z <= last - z
    edge = jnp.minimum(z, last - z)

    def x_part(block):
        if by_slice:
            return x_ref.at[:, pl.ds(pl.multiple_of(block * rows, rows), rows)]
        return x_ref.at[block]

    def g_part(c):
        return g_ref.at[:, pl.ds(pl.multiple_of(c * COLS, COLS), COLS)]

    def x_local(d):
        return pltpu.make_async_copy(
            x_part(2 * d + y), xb.at[d, pl.ds(0, tok)], sx_loc.at[d])

    def x_remote(d):
        return pltpu.make_async_remote_copy(
            src_ref=x_part(2 * d + 1 - y), dst_ref=xb.at[d, pl.ds(tok, tok)],
            send_sem=sx_send.at[d], recv_sem=sx_recv.at[d],
            device_id=mate, device_id_type=MESH)

    def g_local(c):
        return pltpu.make_async_copy(g_part(c), gb.at[c, pl.ds(0, tok)], sg_loc.at[c])

    def g_remote(c):
        return pltpu.make_async_remote_copy(
            src_ref=g_part(c), dst_ref=gb.at[c, pl.ds(tok, tok)],
            send_sem=sg_send.at[c], recv_sem=sg_recv.at[c],
            device_id=mate, device_id_type=MESH)

    def hop(slots, send, recv, d, c, i, target):
        return pltpu.make_async_remote_copy(
            src_ref=slots.at[d, c], dst_ref=slots.at[d, c],
            send_sem=send.at[i % DEPTH], recv_sem=recv.at[d, c],
            device_id=target, device_id_type=MESH)

    def up_hop(i):
        return hop(up, up_send, up_recv, last - i // chunks, i % chunks, i, above)

    def down_hop(i):
        return hop(down, down_send, down_recv, i // chunks, i % chunks, i, below)

    fb_copy = pltpu.make_async_copy(fb_ref.at[0], acc, sf_loc)

    barrier = pltpu.get_barrier_semaphore()
    pl.semaphore_signal(barrier, inc=1, device_id=mate, device_id_type=MESH)
    pl.semaphore_signal(barrier, inc=1, device_id=twin, device_id_type=MESH)

    @pl.when(z < last)
    def _():
        pl.semaphore_signal(barrier, inc=1, device_id=above, device_id_type=MESH)

    @pl.when(z > 0)
    def _():
        pl.semaphore_signal(barrier, inc=1, device_id=below, device_id_type=MESH)

    pl.semaphore_wait(
        barrier, 2 + jnp.where(z < last, 1, 0) + jnp.where(z > 0, 1, 0))

    def start_x(d):
        x_remote(d).start()
        x_local(d).start()

    def start_g(c):
        g_remote(c).start()
        g_local(c).start()

    first = jnp.where(lower, last, 0)
    second = jnp.where(lower, 0, last)
    start_x(first)
    start_g(0)

    @pl.when(edge > 0)
    def _():
        start_x(second)

    @pl.loop(1, chunks)
    def _(c):
        start_g(c)

    @pl.loop(1, last)
    def _(k):
        @pl.when(last - k > z)
        def _():
            start_x(last - k)

        @pl.when(k < z)
        def _():
            start_x(k)

    start_x(z)
    fb_copy.start()

    def wait_x(d):
        x_local(d).wait()
        x_remote(d).wait()
        xt[d] = jnp.swapaxes(xb[d], 0, 1)

    def term(d, c):
        return jnp.dot(xt[d], gb[c], preferred_element_type=jnp.float32) * scale

    def relay(slots, make, sends, i, d, c, inner):
        @pl.when(c == 0)
        def _():
            wait_x(d)

        value = term(d, c)

        @pl.when(i >= DEPTH)
        def _():
            make(i - DEPTH).wait_send()

        @pl.when(inner)
        def _():
            make(i).wait_recv()
            slots[d, c] = (value + slots[d, c].astype(jnp.float32)).astype(slots.dtype)

        @pl.when(jnp.logical_not(inner))
        def _():
            slots[d, c] = value.astype(slots.dtype)

        make(i).start()

    left[...] = jnp.zeros_like(left)

    def out_copy(c):
        view = pl.ds(pl.multiple_of(c * COLS, COLS), COLS)
        return pltpu.make_async_copy(
            acc.at[:, view], out_ref.at[:, view], out_sem.at[c])

    def settle(c):
        @pl.when(c == 0)
        def _():
            wait_x(z)
            fb_copy.wait()

        view = pl.ds(pl.multiple_of(c * COLS, COLS), COLS)
        acc[:, view] += term(z, c)

        @pl.when(z > 0)
        def _():
            up_hop((last - z) * chunks + c).wait_recv()
            acc[:, view] += up[z, c].astype(jnp.float32)

        @pl.when(z < last)
        def _():
            down_hop(z * chunks + c).wait_recv()
            acc[:, view] += down[z, c].astype(jnp.float32)

        out_copy(c).start()
        hi, lo = halves(acc[:, view])
        lanes = pl.ds(pl.multiple_of(c * COLS % WIDE, COLS), COLS)
        high[c * COLS // WIDE, :, lanes] = hi
        low[c * COLS // WIDE, :, lanes] = lo
        member = c // per
        part = f_ref[0, member, :, pl.ds(pl.multiple_of(c % per * COLS, COLS), COLS)]
        wide = jnp.concatenate(
            [jnp.where(member == m, part, 0.0) for m in range(members)], axis=0)
        f_hi, f_lo = halves(wide)
        left[...] += dot_t(hi, f_hi) + dot_t(hi, f_lo) + dot_t(lo, f_hi)

    settle_at = jnp.where(
        edge > 0,
        jnp.maximum((last - z) * chunks + z, z * chunks + last - z),
        (last - 1) * chunks)

    @pl.loop(edge, last * chunks + last)
    def _(t):
        @pl.when(t - edge < chunks)
        def _():
            g_local(t - edge).wait()
            g_remote(t - edge).wait()

        i = t - z

        @pl.when(jnp.logical_and(i >= 0, i < (last - z) * chunks))
        def _():
            relay(up, up_hop, up_send, i, last - i // chunks, i % chunks, z > 0)

        j = t - (last - z)

        @pl.when(jnp.logical_and(j >= 0, j < z * chunks))
        def _():
            relay(down, down_hop, down_send, j, j // chunks, j % chunks, z < last)

        own = t - settle_at

        @pl.when(jnp.logical_and(own >= 0, own < chunks))
        def _():
            settle(own)

    left_copy = pltpu.make_async_remote_copy(
        src_ref=left, dst_ref=left_in, send_sem=left_send, recv_sem=left_recv,
        device_id=twin, device_id_type=MESH)
    left_copy.start()
    left_copy.wait()
    total = left[...] + left_in[...]
    gram = lax.dot_general(
        total, total, (((0,), (0,)), ((), ())),
        precision=lax.Precision.HIGHEST, preferred_element_type=jnp.float32)
    empty = jnp.zeros((rank, rank), jnp.float32)
    inverse = jnp.concatenate([
        jnp.concatenate([
            inverse_factor(gram[m * rank : (m + 1) * rank, m * rank : (m + 1) * rank])
            if m == n else empty for n in range(members)], axis=1)
        for m in range(members)], axis=0)
    basis = lax.dot_general(
        total, inverse, (((1,), (1,)), ((), ())),
        precision=lax.Precision.HIGHEST, preferred_element_type=jnp.float32)
    b_hi, b_lo = halves(jnp.swapaxes(basis, 0, 1))
    for m in range(members):
        span = slice(m * rank, (m + 1) * rank)
        b3_ref[m] = jnp.concatenate([b_hi[span], b_hi[span], b_lo[span]], axis=0)

    def fresh_copy(c):
        return pltpu.make_async_remote_copy(
            src_ref=fresh.at[c], dst_ref=fresh_in.at[c],
            send_sem=fresh_send.at[c], recv_sem=fresh_recv.at[c],
            device_id=twin, device_id_type=MESH)

    wide_count = high.shape[0]
    wide_per = wide_count // members

    @pl.loop(0, wide_count)
    def _(c):
        both = b3_ref[c // wide_per]
        top = jnp.dot(both[rank:], high[c], preferred_element_type=jnp.float32)
        rest = jnp.dot(both[:rank], low[c], preferred_element_type=jnp.float32)
        fresh[c] = top[:rank] + top[rank:] + rest
        fresh_copy(c).start()

    for c in range(wide_count):
        fresh_copy(c).wait()
        view = slice(c % wide_per * WIDE, (c % wide_per + 1) * WIDE)
        fresh_ref[0, c // wide_per, :, view] = fresh[c] + fresh_in[c]

    @pl.loop(0, DEPTH)
    def _(k):
        @pl.when(z < last)
        def _():
            up_hop((last - z) * chunks - DEPTH + k).wait_send()

        @pl.when(z > 0)
        def _():
            down_hop(z * chunks - DEPTH + k).wait_send()

    @pl.loop(0, chunks)
    def _(c):
        out_copy(c).wait()


def compress(features, cotangents, feedback, factors, scale):
    shard_count = lax.axis_size("shard")
    lines = shard_count // 2
    tok, width = cotangents.shape
    rows = features.shape[1] // shard_count
    members, rank = factors.shape[1:3]
    chunks = width // COLS
    by_slice = rows % 128 == 0
    if not by_slice:
        features = features.reshape(tok, shard_count, rows).transpose(1, 0, 2)
    dma = pltpu.SemaphoreType.DMA
    bf16, f32 = jnp.bfloat16, jnp.float32
    flops = 2 * tok * rows * shard_count * width
    vmem = pl.BlockSpec(memory_space=pltpu.VMEM)
    anywhere = pl.BlockSpec(memory_space=pl.ANY)
    return pl.pallas_call(
        functools.partial(merge_kernel, lines, scale, by_slice),
        out_shape=[
            jax.ShapeDtypeStruct((rows, width), f32),
            jax.ShapeDtypeStruct(factors.shape, f32),
            jax.ShapeDtypeStruct((members, 3 * rank, rows), bf16),
        ],
        in_specs=[anywhere] * 3 + [vmem],
        out_specs=[anywhere, vmem, vmem],
        scratch_shapes=[
            pltpu.VMEM((lines, 2 * tok, rows), bf16),
            pltpu.VMEM((lines, rows, 2 * tok), bf16),
            pltpu.VMEM((chunks, 2 * tok, COLS), bf16),
            pltpu.VMEM((lines, chunks, rows, COLS), bf16),
            pltpu.VMEM((lines, chunks, rows, COLS), bf16),
            pltpu.VMEM((rows, width), f32),
            pltpu.VMEM((width // WIDE, rows, WIDE), bf16),
            pltpu.VMEM((width // WIDE, rows, WIDE), bf16),
            pltpu.VMEM((rows, members * rank), f32),
            pltpu.VMEM((rows, members * rank), f32),
            pltpu.VMEM((width // WIDE, rank, WIDE), f32),
            pltpu.VMEM((width // WIDE, rank, WIDE), f32),
            dma, dma, dma((width // WIDE,)), dma((width // WIDE,)),
            dma((lines,)), dma((chunks,)), dma,
            dma((lines,)), dma((lines,)), dma((chunks,)), dma((chunks,)),
            dma((DEPTH,)), dma((lines, chunks)), dma((DEPTH,)), dma((lines, chunks)),
            dma((chunks,)),
        ],
        compiler_params=pltpu.CompilerParams(
            collective_id=0, has_side_effects=True, vmem_limit_bytes=58 * 2**20),
        cost_estimate=pl.CostEstimate(
            flops=flops, bytes_accessed=20 * 2**20, transcendentals=0),
    )(features, cotangents, feedback, factors)


def spread_kernel(replica_count, b3_ref, fresh_ref, merged_ref, update_ref, rest_ref, next_ref):
    value = fresh_ref[...]
    next_ref[...] = value
    hi, lo = halves(value[0, 0])
    product = lax.dot_general(
        b3_ref[0], jnp.concatenate([hi, lo, hi], axis=0), (((0,), (0,)), ((), ())),
        preferred_element_type=jnp.float32)
    update = product / replica_count
    update_ref[...] = update
    rest_ref[0] = merged_ref[...] - update


def spread(b3, fresh, merged, replica_count):
    rows, width = merged.shape
    rank, kv_width = fresh.shape[2:]
    per = kv_width // WIDE
    cols = pl.BlockSpec((rows, WIDE), lambda c: (0, c))
    right = pl.BlockSpec((1, 1, rank, WIDE), lambda c: (0, c // per, 0, c % per))
    return pl.pallas_call(
        functools.partial(spread_kernel, replica_count),
        grid=(width // WIDE,),
        out_shape=[
            jax.ShapeDtypeStruct((rows, width), jnp.float32),
            jax.ShapeDtypeStruct((1, rows, width), jnp.float32),
            jax.ShapeDtypeStruct(fresh.shape, jnp.float32),
        ],
        in_specs=[
            pl.BlockSpec((1,) + b3.shape[1:], lambda c: (c // per, 0, 0)),
            right,
            cols,
        ],
        out_specs=[cols, pl.BlockSpec((1, rows, WIDE), lambda c: (0, 0, c)), right],
        compiler_params=pltpu.CompilerParams(vmem_limit_bytes=58 * 2**20),
    )(b3, fresh, merged)


def body(features, cotangents, feedback, factors):
    grad_scale = 0.25 / math.sqrt(features.shape[0] * lax.axis_size("shard"))
    merged, fresh, b3 = compress(
        features, cotangents, feedback, factors, grad_scale)
    update, new_feedback, next_factors = spread(
        b3, fresh, merged, lax.axis_size("replica"))
    return (update, new_feedback, next_factors)


def solution(mesh):
    return jax.shard_map(
        body,
        mesh=mesh,
        in_specs=(
            P(("groups", "shard", "replica"), None),
            P(("groups", "shard", "replica"), None),
            P("replica", ("groups", "shard"), None),
            P(("groups", "shard"), None, None, None),
        ),
        out_specs=(
            P(("groups", "shard"), None),
            P("replica", ("groups", "shard"), None),
            P(("groups", "shard"), None, None, None),
        ),
        check_vma=False,
    )
```
